512 devices in a mesh: group: 16 (over y, core), seq: 32 (over x, z).
Axes of the slice: x: 4, y: 8, z: 8, core: 2. Of those that a mesh axis runs over, the one named last changes fastest.
Arguments:
- cand_x: bfloat16 [65536, 1024], P(('group', 'seq')), may hold values from -6 to 6
- in_weight: bfloat16 [1024, 4096], P(None, 'group'), may hold values from -0.1875 to 0.1875
- out_weight: bfloat16 [1024, 1024], P('group'), may hold values from -0.1875 to 0.1875
- in_gain: float32 [1024], replicated, may hold values from 0.25 to 1.75
- out_gain: float32 [1024], replicated, may hold values from 0.25 to 1.75
- cache_kv: bfloat16 [2, 128, 2048, 1024], P(None, 'group', 'seq'), may hold values from -6 to 6
- hist_len: int32 [128], P('group'), may hold values from 128 to 2048, as said below
- owner: int32 [16, 32], P('group'), may hold values from 0 to 7, as said below
Outputs:
- mixed: bfloat16 [65536, 1024], P(('group', 'seq'))
The draws below stay inside these ranges and needn't reach their ends.
Inputs may be any that keep to these rules, and one draw needn't show every extreme that they name: `hist_len`: multiples of 128; some request has all 2048 slots live. `owner`: in each group every request index appears exactly four times.
All inputs are finite; a program needn't handle non-finite values.
Results may differ from the reference program's by a relative error of at most 0.0056.
Values may be sent and summed in bfloat16 or wider, within the bound.
A program may use at most 128 MiB of HBM per device.

```python
import jax
import jax.numpy as jnp
from jax import lax

D = 1024
HEADS = 8
HIST = 2048
REQUESTS = 128
CANDS = 65536
N_GROUP = 16
N_SEQ = 32


def draw_hist_len(key, part):
    key = jax.random.fold_in(key, 11)
    first_key, second_key = jax.random.split(key)
    total_requests = N_GROUP * (N_SEQ // 4)
    blocks = jax.random.randint(first_key, (total_requests,), 1, HIST // 128 + 1)
    longest = jax.random.randint(second_key, (), 0, total_requests)
    blocks = jnp.where(jnp.arange(total_requests) == longest, HIST // 128, blocks)
    return (blocks * 128).astype(jnp.int32)


def draw_owner(key, part):
    key = jax.random.fold_in(key, 23)
    group_keys = jax.random.split(key, N_GROUP)
    slots = jax.vmap(lambda single: jax.random.permutation(single, N_SEQ))(group_keys)
    return (slots // 4).astype(jnp.int32)


def block_scale(rng, extent, shards, least, largest):
    level = 1.0
    for position, parts in shards:
        draws = jax.random.uniform(jax.random.fold_in(jax.random.fold_in(rng, 6), position), (parts,), jnp.float32, least / len(shards), largest / len(shards))
        level = level * jnp.repeat(jnp.exp(draws), extent[position] // parts).reshape((-1,) + (1,) * (len(extent) - 1 - position))
    return level


def gaussian(key, dims, scale, most, shards=(), kind=jnp.bfloat16):
    values = jax.random.normal(key, dims, jnp.float32) * scale
    if len(shards) > 0:
        values = block_scale(key, dims, shards, -0.22, 0.18) * values
    return jnp.clip(values, min=-most, max=most).astype(kind)


def setup_inputs(seed: int = 0) -> dict:
    keys = jax.random.split(jax.random.key(seed), 9)
    cand_x = gaussian(keys[0], (CANDS, D), 1.0, 6.0, ((0, 512),))
    in_weight = gaussian(keys[1], (D, 4 * D), D ** -0.5, 0.1875, ((1, 16),))
    out_weight = gaussian(keys[2], (D, D), D ** -0.5, 0.1875, ((0, 16),))
    in_gain = jnp.clip(1.0 + 0.15 * jax.random.normal(keys[3], (D,), jnp.float32), 0.25, 1.75)
    out_gain = jnp.clip(1.0 + 0.15 * jax.random.normal(keys[4], (D,), jnp.float32), 0.25, 1.75)
    cache_kv = gaussian(keys[5], (2, REQUESTS, HIST, D), 1.0, 6.0, ((1, 16), (2, 32)))
    hist_len = draw_hist_len(jax.random.fold_in(keys[8], 71), 0)
    owner = draw_owner(jax.random.fold_in(keys[8], 71), 0)
    return {"cand_x": cand_x, "in_weight": in_weight, "out_weight": out_weight, "in_gain": in_gain, "out_gain": out_gain, "cache_kv": cache_kv, "hist_len": hist_len, "owner": owner}


def layer_norm(values_in, gain):
    values_in = values_in.astype(jnp.float32)
    centre = lax.optimization_barrier(jnp.mean(values_in, axis=-1, keepdims=True))
    centred = values_in - centre
    spread = lax.optimization_barrier(jnp.mean(centred * centred, axis=-1, keepdims=True))
    return centred * lax.rsqrt(spread + 1e-05) * gain.astype(jnp.float32)

def device_rows(tok_x, in_weight, out_weight, in_gain, out_gain, history, length):
    row_count = tok_x.shape[0]
    head_size = D // HEADS
    factor = 1.0 / head_size ** 0.5
    normed = layer_norm(tok_x, in_gain).astype(jnp.bfloat16)
    project = jax.nn.silu(jnp.dot(normed, in_weight, preferred_element_type=jnp.float32)).astype(jnp.bfloat16)
    gate_u = project[:, :D].astype(jnp.float32)
    own_v = project[:, D:2 * D].astype(jnp.float32).reshape(row_count, HEADS, head_size)
    query = project[:, 2 * D:3 * D].astype(jnp.float32).reshape(row_count, HEADS, head_size)
    own_k = project[:, 3 * D:].astype(jnp.float32).reshape(row_count, HEADS, head_size)
    key_heads = history[0].astype(jnp.float32).reshape(HIST, HEADS, head_size)
    value_heads = history[1].astype(jnp.float32).reshape(HIST, HEADS, head_size)
    scores = jnp.einsum('qhd,khd->hqk', query, key_heads) * factor
    live = (jnp.arange(HIST, dtype=jnp.int32) < length).astype(jnp.float32)
    weights = (jax.nn.silu(scores) * live[None, None, :]).astype(jnp.bfloat16)
    attended = jnp.einsum('hqk,khd->qhd', weights.astype(jnp.float32), value_heads)
    own_score = lax.optimization_barrier(jnp.sum(query * own_k, axis=-1)) * factor
    attended = attended + jax.nn.silu(own_score)[:, :, None] * own_v
    gated = (layer_norm(attended.reshape(row_count, D), out_gain) * gate_u).astype(jnp.bfloat16)
    result = tok_x.astype(jnp.float32) + jnp.dot(gated, out_weight, preferred_element_type=jnp.float32)
    return result.astype(jnp.bfloat16)

def reference(cand_x, in_weight, out_weight, in_gain, out_gain, cache_kv, hist_len, owner):
    group_count = owner.shape[0]
    seq_count = owner.shape[1]
    row_count = cand_x.shape[0] // (group_count * seq_count)

    def one_device(index):
        group_at = index // seq_count
        seq_at = index % seq_count
        request = (group_at * (seq_count // 4) + owner[group_at, seq_at]).astype(jnp.int32)
        tok_x = lax.dynamic_slice_in_dim(cand_x, (index * row_count).astype(jnp.int32), row_count, 0)
        history = lax.dynamic_index_in_dim(cache_kv, request, 1, keepdims=False)
        length = hist_len[request]
        return device_rows(tok_x, in_weight, out_weight, in_gain, out_gain, history, length)
    outputs = lax.map(one_device, jnp.arange(group_count * seq_count, dtype=jnp.int32))
    return outputs.reshape(-1, D)
```

```python
import math

import jax
import jax.numpy as jnp
from jax import lax
from jax.experimental import pallas as pl
from jax.experimental.pallas import tpu as pltpu
from jax.sharding import PartitionSpec as P

HEADS = 8
HEAD = 128
NY, NX, NZ = 8, 4, 8
QSPLIT = 4
ROWS = 128
D = 1024
BLOCK = 256
SLOTS = 64
REQ = 8


def silu(v):
    half = 0.5 * v
    return half + half * jnp.tanh(half)


def layer_norm(values_in, gain):
    centre = jnp.mean(values_in, axis=-1, keepdims=True)
    centred = values_in - centre
    spread = jnp.mean(centred * centred, axis=-1, keepdims=True)
    return centred * lax.rsqrt(spread + 1e-05) * gain


def kernel(cand_ref, inw_ref, outw_ref, ing_ref, outg_ref, cache_ref, len_ref, owner_ref, out_ref, *scratch):
    kvs = scratch[:HEADS]
    (win, wout, nbuf, qbuf, ubuf, snd, rcv, acc,
     lk, lw, xs, xr, zs, zr, qs, qr, qcs, qcr, ys, yr, ycs, ycr, ss, rs) = scratch[HEADS:]
    g = lax.axis_index("group")
    s = lax.axis_index("seq")
    y, c = g // 2, g % 2
    x, z = s // NZ, s % NZ
    factor = 1.0 / math.sqrt(HEAD)

    def at_y(yy):
        return {"group": lax.rem(yy + NY, NY) * 2 + c}

    def at_x(xx):
        return {"seq": lax.rem(xx + NX, NX) * NZ + z}

    def at_z(zz):
        return {"seq": x * NZ + lax.rem(zz + NZ, NZ)}

    partner = {"group": y * 2 + 1 - c}
    y_peer = (at_y(y + 1), at_y(y - 1))
    x_peer = (at_x(x + 1), at_x(x - 1))
    z_peer = (at_z(z + 1), at_z(z - 1))

    def remote(src, dst, send, recv, device):
        return pltpu.make_async_remote_copy(src, dst, send, recv, device_id=device, device_id_type=pl.DeviceIdType.MESH)

    def local_kv(h):
        return pltpu.make_async_copy(
            cache_ref.at[:, :, :, pl.ds(h * HEAD, HEAD)], kvs[h].at[:, :, x], lk.at[h]
        )

    own_win = pltpu.make_async_copy(inw_ref, win.at[g], lw.at[0])
    own_wout = pltpu.make_async_copy(outw_ref, wout.at[g], lw.at[1])
    for h in range(HEADS):
        local_kv(h).start()
    own_win.start()
    own_wout.start()

    barrier = pltpu.get_barrier_semaphore()
    for peer in (partner,) + y_peer + x_peer + tuple(at_z(z + k) for k in range(1, NZ)):
        pl.semaphore_signal(barrier, inc=1, device_id=peer, device_id_type=pl.DeviceIdType.MESH)

    nbuf[pl.ds(pl.multiple_of(z * ROWS, ROWS), ROWS), :] = layer_norm(
        cand_ref[...].astype(jnp.float32), ing_ref[...]
    ).astype(jnp.bfloat16)
    for h in range(HEADS):
        local_kv(h).wait()
    own_win.wait()
    own_wout.wait()
    pl.semaphore_wait(barrier, 5 + NZ - 1)

    def x_first(h, way):
        ref = kvs[h].at[:, :, x]
        return remote(ref, ref, xs.at[h, way], xr.at[h, way], x_peer[way])

    def x_second(h, way):
        block = lax.rem(x + (NX - 1 if way == 0 else 1), NX)
        ref = kvs[h].at[way, :, block]
        return remote(ref, ref, xs.at[h, 2 + way], xr.at[h, 2 + way], x_peer[way])

    def x_handle(h):
        for way in range(2):
            block = lax.rem(x + (NX - 1 if way == 0 else 1), NX)
            ref = kvs[h].at[:, :, block]
            remote(ref, ref, xs.at[h, way], xr.at[h, way], x_peer[way]).wait_recv()
            x_second(h, way).start()
        if h + 2 < HEADS:
            for way in range(2):
                x_first(h + 2, way).start()

    def x_complete(h):
        block = lax.rem(x + 2, NX)
        for way in range(2):
            ref = kvs[h].at[way, :, block]
            remote(ref, ref, xs.at[h, 2 + way], xr.at[h, 2 + way], x_peer[way]).wait_recv()

    def z_copy(hop, part, way):
        block = lax.rem(z + (NZ - hop if way == 0 else hop), NZ)
        start = pl.multiple_of(block * ROWS + part * (ROWS // 2), ROWS // 2)
        ref = nbuf.at[pl.ds(start, ROWS // 2), :]
        return remote(ref, ref, zs.at[min(hop, 3), part, way], zr.at[min(hop, 3), part, way], z_peer[way])

    def z_arrival(hop, part, way):
        block = lax.rem(z + (NZ - hop if way == 0 else hop), NZ)
        start = pl.multiple_of(block * ROWS + part * (ROWS // 2), ROWS // 2)
        ref = nbuf.at[pl.ds(start, ROWS // 2), :]
        return remote(ref, ref, zs.at[hop - 1, part, way], zr.at[hop - 1, part, way], z_peer[way])

    def z_sends(hop, part, way):
        return hop < 3 or (hop == 3 and part == way)

    def z_handle(hop, part):
        for way in range(2):
            if hop < 4 or part == way:
                z_arrival(hop, part, way).wait_recv()
            if z_sends(hop, part, way):
                z_copy(hop, part, way).start()

    QROWS = D // QSPLIT

    def q_ref(b, part, core):
        return win.at[2 * b + core, pl.ds(part * QROWS, QROWS), :]

    def q_right(b, part):
        d = lax.rem(y - b + NY, NY)
        return (d <= 2) | (d == 3) if part < QSPLIT // 2 else d <= 2

    def q_left(b, part):
        e = lax.rem(b - y + NY, NY)
        return (e <= 2) | (e == 3) if part >= QSPLIT // 2 else e <= 2

    def q_copy(b, part, way):
        ref = q_ref(b, part, c)
        return remote(ref, ref, qs.at[b - 4, part, way], qr.at[b - 4, part], y_peer[way])

    def q_cross(b, part):
        ref = q_ref(b, part, c)
        return remote(ref, ref, qcs.at[b - 4, part], qcr.at[b - 4, part], partner)

    def q_handle(b, part):
        @pl.when(y != b)
        def _():
            q_copy(b, part, 0).wait_recv()

        @pl.when(q_right(b, part))
        def _():
            q_copy(b, part, 0).start()

        @pl.when(q_left(b, part))
        def _():
            q_copy(b, part, 1).start()

        q_cross(b, part).start()

    def q_cross_arrival(b, part):
        ref = q_ref(b, part, 1 - c)
        remote(ref, ref, qcs.at[b - 4, part], qcr.at[b - 4, part], partner).wait_recv()

    def w_ref(block, piece):
        if piece == 2:
            return wout.at[block]
        return win.at[block, pl.ds(piece * (D // 2), D // 2), :]

    def y_block(hop, way):
        return lax.rem(y + (NY - hop if way == 0 else hop), NY)

    def y_guard(hop, piece, way):
        b = y_block(hop, way)
        return (b != 4) & (b != 5) if piece < 2 else y >= 0

    def y_sends(hop, piece, way):
        return hop < 3 or (hop == 3 and (piece == 1) == (way == 1))

    def y_copy(hop, piece, way):
        ref = w_ref(2 * y_block(hop, way) + c, piece)
        return remote(ref, ref, ys.at[hop, piece, way], yr.at[hop, piece, way], y_peer[way])

    def y_arrival(hop, piece, way):
        ref = w_ref(2 * y_block(hop, way) + c, piece)
        return remote(ref, ref, ys.at[hop - 1, piece, way], yr.at[hop - 1, piece, way], y_peer[way])

    def y_cross(b, piece):
        ref = w_ref(2 * b + c, piece)
        return remote(ref, ref, ycs.at[b, piece], ycr.at[b, piece], partner)

    def y_cross_arrival(b, piece):
        ref = w_ref(2 * b + 1 - c, piece)
        remote(ref, ref, ycs.at[b, piece], ycr.at[b, piece], partner).wait_recv()

    def y_handle(hop, piece):
        for way in range(2):
            if hop == 4 and (piece == 1) != (way == 1):
                continue

            @pl.when(y_guard(hop, piece, way))
            def _():
                y_arrival(hop, piece, way).wait_recv()
                if y_sends(hop, piece, way):
                    y_copy(hop, piece, way).start()
                y_cross(y_block(hop, way), piece).start()

    early = ((y <= 3), (y <= 1) | (y >= 6))

    def y_own(first):
        for piece in range(3):
            for way in range(2):
                chosen = early[way] if first else jnp.logical_not(early[way])

                @pl.when(chosen & y_guard(0, piece, way))
                def _():
                    y_copy(0, piece, way).start()

    def queries(block):
        @pl.loop(0, NZ // 2)
        def _(i):
            rows = pl.ds(pl.multiple_of(i * 2 * ROWS, 2 * ROWS), 2 * ROWS)
            value = jnp.dot(nbuf[rows, :], win[2 * 4 + block], preferred_element_type=jnp.float32)
            qbuf[rows, block * BLOCK : (block + 1) * BLOCK] = silu(value).astype(jnp.bfloat16)

    column = lax.broadcasted_iota(jnp.int32, (1, NX * SLOTS), 1)
    slot = (column // SLOTS * NZ + z) * SLOTS + column % SLOTS

    def send_partial(h, dest):
        return remote(snd.at[h, dest], rcv.at[h, z], ss.at[h, dest], rs.at[h, z], at_z(dest))

    def attend(h):
        kv = kvs[h]

        @pl.loop(0, NZ)
        def _(i):
            step = (i + 1) // 2
            dest = lax.rem(z + 4 + NZ + (1 - 2 * (i % 2)) * step, NZ)
            request = owner_ref[0, x * NZ + dest]
            length = len_ref[request]
            query = qbuf[pl.ds(pl.multiple_of(dest * ROWS, ROWS), ROWS), h * HEAD : (h + 1) * HEAD]
            keys = kv[0, request].reshape(NX * SLOTS, HEAD)
            values = kv[1, request].reshape(NX * SLOTS, HEAD)
            scores = lax.dot_general(
                query, keys, (((1,), (1,)), ((), ())), preferred_element_type=jnp.float32
            )
            weights = jnp.where(slot < length, silu(scores * factor), 0.0).astype(jnp.bfloat16)
            part = jnp.dot(weights, values, preferred_element_type=jnp.float32)
            snd[h, dest] = part.astype(jnp.bfloat16)

            @pl.when(i < NZ - 1)
            def _():
                send_partial(h, dest).start()

    def collect(h):
        total = acc[:, h * HEAD : (h + 1) * HEAD] + snd[h, z].astype(jnp.float32)
        for k in range(1, NZ):
            src = lax.rem(z + k, NZ)
            remote(snd.at[h, src], rcv.at[h, src], ss.at[h, src], rs.at[h, src], at_z(src)).wait_recv()
            total = total + rcv[h, src].astype(jnp.float32)
        acc[:, h * HEAD : (h + 1) * HEAD] = total

    def own_rows():
        rows = pl.ds(pl.multiple_of(z * ROWS, ROWS), ROWS)
        mine = nbuf[rows, :]

        def project(block):
            value = jnp.dot(mine, win[block], preferred_element_type=jnp.float32)
            return silu(value).astype(jnp.bfloat16)

        for j in range(4):
            columns = slice(j * BLOCK, (j + 1) * BLOCK)
            ubuf[:, columns] = project(j)
            own_v = project(4 + j).astype(jnp.float32)
            own_k = project(12 + j).astype(jnp.float32)
            product = qbuf[rows, columns].astype(jnp.float32) * own_k
            for t in range(BLOCK // HEAD):
                part = slice(t * HEAD, (t + 1) * HEAD)
                score = jnp.sum(product[:, part], axis=-1, keepdims=True) * factor
                acc[:, j * BLOCK + t * HEAD : j * BLOCK + (t + 1) * HEAD] = silu(score) * own_v[:, part]

    for h in range(2):
        for way in range(2):
            x_first(h, way).start()
    for part in range(2):
        for way in range(2):
            z_copy(0, part, way).start()
    y_own(True)
    for piece in range(3):
        @pl.when(y_guard(0, piece, 0))
        def _():
            y_cross(y, piece).start()

    for i in range(8):
        q_handle(4 + i // QSPLIT, i % QSPLIT)
        z_handle(1 + i // 2, i % 2)
        if i in (2, 5):
            x_handle(i // 3)
    y_own(False)
    for part in range(QSPLIT):
        q_cross_arrival(4, part)
    queries(0)
    queries(1)
    x_handle(2)
    x_complete(0)
    attend(0)
    x_complete(1)
    attend(1)
    for piece in range(3):
        y_handle(1, piece)
    x_handle(3)
    x_complete(2)
    attend(2)
    for part in range(QSPLIT):
        q_cross_arrival(5, part)
    queries(2)
    queries(3)
    for piece in range(3):
        y_handle(2, piece)
    x_handle(4)
    x_complete(3)
    attend(3)
    for piece in range(3):
        y_handle(3, piece)
    x_handle(5)
    x_complete(4)
    attend(4)
    for piece in range(3):
        y_handle(4, piece)
    x_handle(6)
    x_complete(5)
    attend(5)
    for b in range(NY):
        if b not in (4, 5):
            y_cross_arrival(b, 0)
            y_cross_arrival(b, 1)
    own_rows()
    x_handle(7)
    x_complete(6)
    attend(6)
    for h in range(6):
        collect(h)
    x_complete(7)
    attend(7)
    for b in range(NY):
        y_cross_arrival(b, 2)
    collect(6)
    collect(7)
    gated = (layer_norm(acc[...], outg_ref[...]) * ubuf[...].astype(jnp.float32)).astype(jnp.bfloat16)
    result = jnp.dot(gated, wout[...].reshape(D, D), preferred_element_type=jnp.float32)
    out_ref[...] = (cand_ref[...].astype(jnp.float32) + result).astype(jnp.bfloat16)

    for h in range(HEADS):
        for way in range(2):
            x_first(h, way).wait_send()
            x_second(h, way).wait_send()
    for hop in range(4):
        for part in range(2):
            for way in range(2):
                if z_sends(hop, part, way):
                    z_copy(hop, part, way).wait_send()
    for b in (4, 5):
        for part in range(QSPLIT):
            q_cross(b, part).wait_send()

            @pl.when(q_right(b, part))
            def _():
                q_copy(b, part, 0).wait_send()

            @pl.when(q_left(b, part))
            def _():
                q_copy(b, part, 1).wait_send()

    for piece in range(3):
        for hop in range(4):
            for way in range(2):
                if y_sends(hop, piece, way):
                    @pl.when(y_guard(hop, piece, way))
                    def _():
                        y_copy(hop, piece, way).wait_send()
        for b in range(NY):
            if piece == 2 or b not in (4, 5):
                y_cross(b, piece).wait_send()

    for h in range(HEADS):
        @pl.loop(1, NZ)
        def _(k):
            send_partial(h, lax.rem(z + k, NZ)).wait_send()


def local(cand_x, in_weight, out_weight, in_gain, out_gain, cache_kv, hist_len, owner):
    bf16, dma = jnp.bfloat16, pltpu.SemaphoreType.DMA
    vmem, anywhere = pl.BlockSpec(memory_space=pltpu.VMEM), pl.BlockSpec(memory_space=pl.ANY)
    smem = pl.BlockSpec(memory_space=pltpu.SMEM)
    return pl.pallas_call(
        kernel,
        out_shape=jax.ShapeDtypeStruct((ROWS, D), bf16),
        in_specs=[vmem, anywhere, anywhere, vmem, vmem, anywhere, smem, smem],
        out_specs=vmem,
        scratch_shapes=[pltpu.VMEM((2, REQ, NX, SLOTS, HEAD), bf16) for _ in range(HEADS)]
        + [
            pltpu.VMEM((2 * NY, D, BLOCK), bf16),
            pltpu.VMEM((2 * NY, D // (2 * NY), D), bf16),
            pltpu.VMEM((NZ * ROWS, D), bf16),
            pltpu.VMEM((NZ * ROWS, D), bf16),
            pltpu.VMEM((ROWS, D), bf16),
            pltpu.VMEM((HEADS, NZ, ROWS, HEAD), bf16),
            pltpu.VMEM((HEADS, NZ, ROWS, HEAD), bf16),
            pltpu.VMEM((ROWS, D), jnp.float32),
            dma((HEADS,)), dma((2,)),
            dma((HEADS, 4)), dma((HEADS, 4)),
            dma((4, 2, 2)), dma((4, 2, 2)),
            dma((2, QSPLIT, 2)), dma((2, QSPLIT)), dma((2, QSPLIT)), dma((2, QSPLIT)),
            dma((4, 3, 2)), dma((4, 3, 2)), dma((NY, 3)), dma((NY, 3)),
            dma((HEADS, NZ)), dma((HEADS, NZ)),
        ],
        compiler_params=pltpu.CompilerParams(
            collective_id=0, has_side_effects=True, vmem_limit_bytes=56 * 1024 * 1024
        ),
        cost_estimate=pl.CostEstimate(flops=5_000_000_000, bytes_accessed=4_000_000, transcendentals=4_000_000),
    )(cand_x, in_weight, out_weight, in_gain[None, :], out_gain[None, :], cache_kv, hist_len, owner)


def solution(mesh):
    placed = (
        P(("group", "seq"), None),
        P(None, "group"),
        P("group", None),
        P(),
        P(),
        P(None, "group", "seq", None),
        P("group"),
        P("group", None),
    )
    return jax.shard_map(
        local, mesh=mesh, in_specs=placed, out_specs=P(("group", "seq"), None), check_vma=False
    )
```

```python
import math

import jax
import jax.numpy as jnp
from jax import lax
from jax.experimental import pallas as pl
from jax.experimental.pallas import tpu as pltpu
from jax.sharding import PartitionSpec as P

HEADS = 8
HEAD = 128
NY, NX, NZ = 8, 4, 8
PIECES = 2
ROWS = 128
D = 1024
BLOCK = 256
SLOTS = 64
REQ = 8
PIECE = D // PIECES
WINDOW = 2
UNROLL = 2
RING = 6


def silu(v):
    half = 0.5 * v
    return half + half * jnp.tanh(half)


def layer_norm(values_in, gain):
    centre = jnp.mean(values_in, axis=-1, keepdims=True)
    centred = values_in - centre
    spread = jnp.mean(centred * centred, axis=-1, keepdims=True)
    return centred * lax.rsqrt(spread + 1e-05) * gain


def kernel(cand_ref, inw_ref, outw_ref, ing_ref, outg_ref, cache_ref, len_ref, owner_ref, out_ref, *scratch):
    kvs = scratch[:HEADS]
    (win, wout, nbuf, qbuf, ubuf, snd, rcv, acc,
     rsb,
     lk, lw, xs, xr, zs, zr, ys, yr, ycs, ycr, qs, qr, qzs, qzr, qcs, qcr, os, orv, ocs, ocr, ss, rs, rss, rsr) = scratch[HEADS:]
    g = lax.axis_index("group")
    s = lax.axis_index("seq")
    y, c = g // 2, g % 2
    x, z = s // NZ, s % NZ
    factor = 1.0 / math.sqrt(HEAD)

    def at_y(yy):
        return {"group": lax.rem(yy + NY, NY) * 2 + c}

    def at_x(xx):
        return {"seq": lax.rem(xx + NX, NX) * NZ + z}

    def at_z(zz):
        return {"seq": x * NZ + lax.rem(zz + NZ, NZ)}

    partner = {"group": y * 2 + 1 - c}
    y_peer = (at_y(y + 1), at_y(y - 1))
    x_peer = (at_x(x + 1), at_x(x - 1))
    z_peer = (at_z(z + 1), at_z(z - 1))

    def remote(src, dst, send, recv, device):
        return pltpu.make_async_remote_copy(src, dst, send, recv, device_id=device, device_id_type=pl.DeviceIdType.MESH)

    def local_kv(h):
        return pltpu.make_async_copy(
            cache_ref.at[:, :, :, pl.ds(h * HEAD, HEAD)], kvs[h].at[:, :, x], lk.at[h]
        )

    has_queries = (y == 4) | (y == 5)
    my_rows = pl.ds(pl.multiple_of(z * ROWS, ROWS), ROWS)
    own_win = pltpu.make_async_copy(inw_ref, win.at[g], lw.at[0])
    own_part = pltpu.make_async_copy(inw_ref.at[my_rows, :], win.at[g, my_rows, :], lw.at[0])

    def own_weights(act):
        @pl.when(has_queries)
        def _():
            act(own_part)

        @pl.when(jnp.logical_not(has_queries))
        def _():
            act(own_win)

    own_wout = pltpu.make_async_copy(outw_ref, wout.at[g], lw.at[1])
    local_kv(0).start()
    local_kv(1).start()
    own_weights(lambda copy: copy.start())
    for h in range(2, HEADS):
        local_kv(h).start()
    own_wout.start()

    barrier = pltpu.get_barrier_semaphore()
    for peer in (partner,) + x_peer + tuple(at_y(y + k) for k in range(1, NY)) + tuple(at_z(z + k) for k in range(1, NZ)):
        pl.semaphore_signal(barrier, inc=1, device_id=peer, device_id_type=pl.DeviceIdType.MESH)

    for h in range(2):
        local_kv(h).wait()
    pl.semaphore_wait(barrier, 3 + NY - 1 + NZ - 1)

    def x_first(h, way):
        ref = kvs[h].at[:, :, x]
        return remote(ref, ref, xs.at[h, way], xr.at[h, way], x_peer[way])

    def x_second(h, way):
        block = lax.rem(x + (NX - 1 if way == 0 else 1), NX)
        ref = kvs[h].at[way, :, block]
        return remote(ref, ref, xs.at[h, 2 + way], xr.at[h, 2 + way], x_peer[way])

    def x_handle(h):
        for way in range(2):
            block = lax.rem(x + (NX - 1 if way == 0 else 1), NX)
            ref = kvs[h].at[:, :, block]
            remote(ref, ref, xs.at[h, way], xr.at[h, way], x_peer[way]).wait_recv()
            x_second(h, way).start()
        if h + WINDOW < HEADS:
            for way in range(2):
                x_first(h + WINDOW, way).start()

    def x_complete(h):
        block = lax.rem(x + 2, NX)
        for way in range(2):
            ref = kvs[h].at[way, :, block]
            remote(ref, ref, xs.at[h, 2 + way], xr.at[h, 2 + way], x_peer[way]).wait_recv()

    def z_copy(hop, part, way):
        block = lax.rem(z + (NZ - hop if way == 0 else hop), NZ)
        start = pl.multiple_of(block * ROWS + part * (ROWS // 2), ROWS // 2)
        ref = nbuf.at[pl.ds(start, ROWS // 2), :]
        return remote(ref, ref, zs.at[min(hop, 3), part, way], zr.at[min(hop, 3), part, way], z_peer[way])

    def z_arrival(hop, part, way):
        block = lax.rem(z + (NZ - hop if way == 0 else hop), NZ)
        start = pl.multiple_of(block * ROWS + part * (ROWS // 2), ROWS // 2)
        ref = nbuf.at[pl.ds(start, ROWS // 2), :]
        return remote(ref, ref, zs.at[hop - 1, part, way], zr.at[hop - 1, part, way], z_peer[way])

    def z_sends(hop, part, way):
        return hop < 3 or (hop == 3 and part == way)

    def z_handle(hop, part):
        for way in range(2):
            if hop < 4 or part == way:
                z_arrival(hop, part, way).wait_recv()
            if z_sends(hop, part, way):
                z_copy(hop, part, way).start()

    def w_ref(b, piece, core):
        return win.at[2 * b + core, pl.ds(piece * PIECE, PIECE), :]

    def y_block(way, hop):
        return lax.rem(y + NY - hop if way == 0 else y + hop, NY)

    def y_sends(way, hop, piece):
        return hop < 3 or (hop == 3 and piece == way)

    def y_copy(way, hop, piece):
        ref = w_ref(y_block(way, hop), piece, c)
        return remote(ref, ref, ys.at[way, hop, piece], yr.at[way, hop, piece], y_peer[way])

    def y_cross(b, piece):
        ref = w_ref(b, piece, c)
        return remote(ref, ref, ycs.at[b, piece], ycr.at[b, piece], partner)

    def y_cross_arrival(b):
        for piece in range(PIECES):
            ref = w_ref(b, piece, 1 - c)
            remote(ref, ref, ycs.at[b, piece], ycr.at[b, piece], partner).wait_recv()

    def y_guard(way, hop):
        b = y_block(way, hop)
        return (b != 4) & (b != 5)

    def y_slot(hop, piece):
        for way in range(2):
            if hop > 0 and not y_sends(way, hop - 1, piece):
                continue

            @pl.when(y_guard(way, hop))
            def _():
                b = y_block(way, hop)
                if hop > 0:
                    ref = w_ref(b, piece, c)
                    remote(ref, ref, ys.at[way, hop - 1, piece], yr.at[way, hop - 1, piece], y_peer[way]).wait_recv()
                if y_sends(way, hop, piece):
                    y_copy(way, hop, piece).start()
                if hop > 0 or way == 0:
                    y_cross(b, piece).start()

    def q_part(b, way, hop):
        block = lax.rem(z + NZ - hop if way == 0 else z + hop, NZ)
        if hop < 3:
            return win.at[2 * b + c, pl.ds(pl.multiple_of(block * ROWS, ROWS), ROWS), :]
        start = pl.multiple_of(block * ROWS + way * (ROWS // 2), ROWS // 2)
        return win.at[2 * b + c, pl.ds(start, ROWS // 2), :]

    def q_far(b, k):
        ref = win.at[2 * b + c, my_rows, :]
        return remote(ref, ref, qs.at[b - 4, k], qr.at[b - 4], at_y(y + k))

    def q_share():
        for b in (4, 5):
            @pl.when(y == b)
            def _():
                for k in (4, 3, 5, 2, 6, 1, 7):
                    q_far(b, k).start()

    def q_copy(b, hop, way):
        ref = q_part(b, way, hop)
        return remote(ref, ref, qzs.at[b - 4, hop, way], qzr.at[b - 4, hop, way], z_peer[way])

    def q_slot(hop):
        for b in (4, 5):
            if hop == 0:
                @pl.when(y != b)
                def _():
                    q_far(b, 1).wait_recv()

            for way in range(2):
                if hop > 0:
                    block = lax.rem(z + NZ - hop if way == 0 else z + hop, NZ)
                    if hop < 4:
                        ref = win.at[2 * b + c, pl.ds(pl.multiple_of(block * ROWS, ROWS), ROWS), :]
                    else:
                        start = pl.multiple_of(block * ROWS + way * (ROWS // 2), ROWS // 2)
                        ref = win.at[2 * b + c, pl.ds(start, ROWS // 2), :]
                    remote(ref, ref, qzs.at[b - 4, hop - 1, way], qzr.at[b - 4, hop - 1, way], z_peer[way]).wait_recv()
                if hop < 4:
                    q_copy(b, hop, way).start()
            if hop == 4:
                q_cross(b).start()

    def q_cross(b):
        ref = win.at[2 * b + c]
        return remote(ref, ref, qcs.at[b - 4], qcr.at[b - 4], partner)

    def q_cross_arrival(b):
        ref = win.at[2 * b + 1 - c]
        remote(ref, ref, qcs.at[b - 4], qcr.at[b - 4], partner).wait_recv()

    def o_copy(way, hop):
        ref = wout.at[2 * y_block(way, hop) + c]
        return remote(ref, ref, os.at[way, hop], orv.at[way, hop], y_peer[way])

    def o_cross(b):
        ref = wout.at[2 * b + c]
        return remote(ref, ref, ocs.at[b], ocr.at[b], partner)

    def o_slot(hop):
        for way in range(2):
            if hop == 4 and way == 1:
                continue
            b = y_block(way, hop)
            if hop > 0:
                ref = wout.at[2 * b + c]
                remote(ref, ref, os.at[way, hop - 1], orv.at[way, hop - 1], y_peer[way]).wait_recv()
            if hop < 3 or (hop == 3 and way == 0):
                o_copy(way, hop).start()
            if hop > 0 or way == 0:
                o_cross(b).start()

    def queries(block):
        @pl.loop(0, NZ // 2)
        def _(i):
            rows = pl.ds(pl.multiple_of(i * 2 * ROWS, 2 * ROWS), 2 * ROWS)
            value = jnp.dot(nbuf[rows, :], win[2 * 4 + block], preferred_element_type=jnp.float32)
            qbuf[rows, block * BLOCK : (block + 1) * BLOCK] = silu(value).astype(jnp.bfloat16)

    column = lax.broadcasted_iota(jnp.int32, (1, NX * SLOTS), 1)
    slot = (column // SLOTS * NZ + z) * SLOTS + column % SLOTS

    def send_partial(h, dest):
        return remote(snd.at[h, dest], rcv.at[h - RING, z], ss.at[h - RING, dest], rs.at[h - RING, z], at_z(dest))

    def attend(h):
        kv = kvs[h]

        def block(i):
            step = (i + 1) // 2
            dest = lax.rem(z + 4 + NZ + (1 - 2 * (i % 2)) * step, NZ)
            request = owner_ref[0, x * NZ + dest]
            length = len_ref[request]
            query = qbuf[pl.ds(pl.multiple_of(dest * ROWS, ROWS), ROWS), h * HEAD : (h + 1) * HEAD]
            keys = kv[0, request].reshape(NX * SLOTS, HEAD)
            values = kv[1, request].reshape(NX * SLOTS, HEAD)
            scores = lax.dot_general(
                query, keys, (((1,), (1,)), ((), ())), preferred_element_type=jnp.float32
            )
            weights = jnp.where(slot < length, silu(scores * factor), 0.0).astype(jnp.bfloat16)
            return dest, jnp.dot(weights, values, preferred_element_type=jnp.float32).astype(jnp.bfloat16)

        @pl.loop(0, NZ // UNROLL)
        def _(j):
            done = [block(j * UNROLL + k) for k in range(UNROLL)]
            for dest, part in done:
                snd[h, dest] = part
            if h >= RING:
                for k, (dest, _) in enumerate(done):
                    if k < UNROLL - 1:
                        send_partial(h, dest).start()
                    else:
                        @pl.when(j < NZ // UNROLL - 1)
                        def _():
                            send_partial(h, dest).start()

        if h < RING:
            ring_step(h, 1)
            pending[h] = 2

    def collect(h):
        total = acc[:, h * HEAD : (h + 1) * HEAD] + snd[h, z].astype(jnp.float32)
        for k in range(1, NZ):
            src = lax.rem(z + k, NZ)
            block = rcv.at[h - RING, src]
            remote(block, block, ss.at[h - RING, src], rs.at[h - RING, src], at_z(src)).wait_recv()
            total = total + rcv[h - RING, src].astype(jnp.float32)
        acc[:, h * HEAD : (h + 1) * HEAD] = total

    pending = {}

    def ring_rows(way, hop):
        return slice(0, ROWS) if hop > 1 else slice(0, ROWS // 2) if way == 0 else slice(ROWS // 2, ROWS)

    def ring_copy(h, hop, way):
        dest = lax.rem(z + 5 - hop if way == 0 else z + NZ - 5 + hop, NZ)
        rows = ring_rows(way, hop)
        return dest, remote(
            snd.at[h, dest, rows], rsb.at[way, h, hop - 1, rows], rss.at[way, h, hop - 1], rsr.at[way, h, hop - 1], z_peer[way]
        )

    def ring_take(h, hop, way):
        rows = ring_rows(way, hop)
        ref = rsb.at[way, h, hop - 1, rows]
        remote(ref, ref, rss.at[way, h, hop - 1], rsr.at[way, h, hop - 1], z_peer[way]).wait_recv()
        return rsb[way, h, hop - 1, rows].astype(jnp.float32)

    def ring_step(h, hop):
        for way in range(2):
            dest, copy = ring_copy(h, hop, way)
            if hop > 1:
                rows = ring_rows(way, hop - 1)
                total = snd[h, dest, rows].astype(jnp.float32) + ring_take(h, hop - 1, way)
                snd[h, dest, rows] = total.astype(jnp.bfloat16)
            copy.start()

    def tick():
        for h in sorted(pending):
            hop = pending[h]
            if hop <= 4:
                ring_step(h, hop)
                pending[h] = hop + 1
            else:
                columns = slice(h * HEAD, (h + 1) * HEAD)
                acc[:, columns] += snd[h, z].astype(jnp.float32) + ring_take(h, 4, 0) + ring_take(h, 4, 1)
                del pending[h]

    def own_rows():
        rows = pl.ds(pl.multiple_of(z * ROWS, ROWS), ROWS)
        mine = nbuf[rows, :]

        def project(block):
            value = jnp.dot(mine, win[block], preferred_element_type=jnp.float32)
            return silu(value).astype(jnp.bfloat16)

        for j in range(4):
            columns = slice(j * BLOCK, (j + 1) * BLOCK)
            ubuf[:, columns] = project(j)
            own_v = project(4 + j).astype(jnp.float32)
            own_k = project(12 + j).astype(jnp.float32)
            product = qbuf[rows, columns].astype(jnp.float32) * own_k
            for t in range(BLOCK // HEAD):
                part = slice(t * HEAD, (t + 1) * HEAD)
                score = jnp.sum(product[:, part], axis=-1, keepdims=True) * factor
                acc[:, j * BLOCK + t * HEAD : j * BLOCK + (t + 1) * HEAD] += silu(score) * own_v[:, part]

    own_weights(lambda copy: copy.wait())
    q_share()
    for h in range(2):
        for way in range(2):
            x_first(h, way).start()
    own_wout.wait()
    y_slot(0, 0)
    o_slot(0)
    nbuf[my_rows, :] = layer_norm(cand_ref[...].astype(jnp.float32), ing_ref[...]).astype(jnp.bfloat16)
    for part in range(2):
        for way in range(2):
            z_copy(0, part, way).start()
    acc[...] = jnp.zeros_like(acc)
    for h in range(2, HEADS):
        local_kv(h).wait()
    z_handle(1, 0)
    y_slot(0, 1)
    z_handle(1, 1)
    z_handle(2, 0)
    x_handle(0)
    q_slot(0)
    z_handle(2, 1)
    y_slot(1, 0)
    z_handle(3, 0)
    q_slot(1)
    z_handle(3, 1)
    x_handle(1)
    z_handle(4, 0)
    q_slot(2)
    y_slot(1, 1)
    z_handle(4, 1)
    q_slot(3)
    y_slot(2, 0)
    x_handle(2)
    q_slot(4)
    o_slot(1)
    y_slot(2, 1)
    q_cross_arrival(4)
    queries(0)
    queries(1)
    x_complete(0)
    attend(0)
    x_handle(3)
    y_slot(3, 0)
    o_slot(2)
    x_complete(1)
    tick()
    attend(1)
    q_cross_arrival(5)
    queries(2)
    queries(3)
    y_slot(3, 1)
    x_complete(2)
    tick()
    attend(2)
    x_handle(4)
    y_slot(4, 0)
    o_slot(3)
    x_complete(3)
    tick()
    attend(3)
    x_handle(5)
    y_slot(4, 1)
    x_complete(4)
    tick()
    attend(4)
    x_handle(6)
    o_slot(4)
    for b in range(NY):
        if b not in (4, 5):
            y_cross_arrival(b)
    own_rows()
    x_complete(5)
    tick()
    attend(5)
    tick()
    x_handle(7)
    for b in range(NY):
        remote(wout.at[2 * b + 1 - c], wout.at[2 * b + 1 - c], ocs.at[b], ocr.at[b], partner).wait_recv()
    tick()
    x_complete(6)
    tick()
    attend(6)
    tick()
    x_complete(7)
    attend(7)
    while pending:
        tick()
    for h in range(RING, HEADS):
        collect(h)
    gated = (layer_norm(acc[...], outg_ref[...]) * ubuf[...].astype(jnp.float32)).astype(jnp.bfloat16)
    result = jnp.dot(gated, wout[...].reshape(D, D), preferred_element_type=jnp.float32)
    out_ref[...] = (cand_ref[...].astype(jnp.float32) + result).astype(jnp.bfloat16)

    for h in range(HEADS):
        for way in range(2):
            x_first(h, way).wait_send()
            x_second(h, way).wait_send()
    for hop in range(4):
        for part in range(2):
            for way in range(2):
                if z_sends(hop, part, way):
                    z_copy(hop, part, way).wait_send()
    for way in range(2):
        for hop in range(4):
            @pl.when(y_guard(way, hop))
            def _():
                for piece in range(PIECES):
                    if y_sends(way, hop, piece):
                        y_copy(way, hop, piece).wait_send()

            if hop < 3 or way == 0:
                o_copy(way, hop).wait_send()
            for b in (4, 5):
                q_copy(b, hop, way).wait_send()
    for b in range(NY):
        o_cross(b).wait_send()
        if b in (4, 5):
            q_cross(b).wait_send()

            @pl.when(y == b)
            def _():
                for k in range(1, NY):
                    q_far(b, k).wait_send()
        else:
            for piece in range(PIECES):
                y_cross(b, piece).wait_send()
    for h in range(RING):
        for hop in range(1, 5):
            for way in range(2):
                ring_copy(h, hop, way)[1].wait_send()

    for h in range(RING, HEADS):
        @pl.loop(1, NZ)
        def _(k):
            send_partial(h, lax.rem(z + k, NZ)).wait_send()


def local(cand_x, in_weight, out_weight, in_gain, out_gain, cache_kv, hist_len, owner):
    bf16, dma = jnp.bfloat16, pltpu.SemaphoreType.DMA
    vmem, anywhere = pl.BlockSpec(memory_space=pltpu.VMEM), pl.BlockSpec(memory_space=pl.ANY)
    smem = pl.BlockSpec(memory_space=pltpu.SMEM)
    return pl.pallas_call(
        kernel,
        out_shape=jax.ShapeDtypeStruct((ROWS, D), bf16),
        in_specs=[vmem, anywhere, anywhere, vmem, vmem, anywhere, smem, smem],
        out_specs=vmem,
        scratch_shapes=[pltpu.VMEM((2, REQ, NX, SLOTS, HEAD), bf16) for _ in range(HEADS)]
        + [
            pltpu.VMEM((2 * NY, D, BLOCK), bf16),
            pltpu.VMEM((2 * NY, D // (2 * NY), D), bf16),
            pltpu.VMEM((NZ * ROWS, D), bf16),
            pltpu.VMEM((NZ * ROWS, D), bf16),
            pltpu.VMEM((ROWS, D), bf16),
            pltpu.VMEM((HEADS, NZ, ROWS, HEAD), bf16),
            pltpu.VMEM((max(HEADS - RING, 1), NZ, ROWS, HEAD), bf16),
            pltpu.VMEM((ROWS, D), jnp.float32),
            pltpu.VMEM((2, max(RING, 1), 4, ROWS, HEAD), bf16),
            dma((HEADS,)), dma((2,)),
            dma((HEADS, 4)), dma((HEADS, 4)),
            dma((4, 2, 2)), dma((4, 2, 2)),
            dma((2, 4, PIECES)), dma((2, 4, PIECES)), dma((NY, PIECES)), dma((NY, PIECES)),
            dma((2, NY)), dma((2,)), dma((2, 4, 2)), dma((2, 4, 2)), dma((2,)), dma((2,)),
            dma((2, 4)), dma((2, 4)), dma((NY,)), dma((NY,)),
            dma((max(HEADS - RING, 1), NZ)), dma((max(HEADS - RING, 1), NZ)),
            dma((2, max(RING, 1), 4)), dma((2, max(RING, 1), 4)),
        ],
        compiler_params=pltpu.CompilerParams(
            collective_id=0, has_side_effects=True, vmem_limit_bytes=56 * 1024 * 1024
        ),
        cost_estimate=pl.CostEstimate(flops=5_000_000_000, bytes_accessed=4_000_000, transcendentals=4_000_000),
    )(cand_x, in_weight, out_weight, in_gain[None, :], out_gain[None, :], cache_kv, hist_len, owner)


def solution(mesh):
    placed = (
        P(("group", "seq"), None),
        P(None, "group"),
        P("group", None),
        P(),
        P(),
        P(None, "group", "seq", None),
        P("group"),
        P("group", None),
    )
    return jax.shard_map(
        local, mesh=mesh, in_specs=placed, out_specs=P(("group", "seq"), None), check_vma=False
    )
```

```python
import math

import jax
import jax.numpy as jnp
from jax import lax
from jax.experimental import pallas as pl
from jax.experimental.pallas import tpu as pltpu
from jax.sharding import PartitionSpec as P

HEADS = 8
HEAD = 128
NY, NX, NZ = 8, 4, 8
PIECES = 2
ROWS = 128
D = 1024
BLOCK = 256
SLOTS = 64
REQ = 8
PIECE = D // PIECES
WINDOW = 3
UNROLL = 2
RING = 2


def silu(v):
    half = 0.5 * v
    return half + half * jnp.tanh(half)


def layer_norm(values_in, gain):
    centre = jnp.mean(values_in, axis=-1, keepdims=True)
    centred = values_in - centre
    spread = jnp.mean(centred * centred, axis=-1, keepdims=True)
    return centred * lax.rsqrt(spread + 1e-05) * gain


def kernel(cand_hbm, inw_ref, outw_ref, ing_ref, outg_ref, cache_ref, len_ref, owner_ref, out_ref, *scratch):
    kvs = scratch[:HEADS]
    (cand_ref, win, wout, nbuf, qbuf, ubuf, snd, rcv, acc,
     rsb,
     lk, lw, xs, xr, zs, zr, ys, yr, ycs, ycr, qs, qr, qzs, qzr, qcs, qcr, os, orv, ocs, ocr, ss, rs, rss, rsr) = scratch[HEADS:]
    g = lax.axis_index("group")
    s = lax.axis_index("seq")
    y, c = g // 2, g % 2
    x, z = s // NZ, s % NZ
    factor = 1.0 / math.sqrt(HEAD)

    def at_y(yy):
        return {"group": lax.rem(yy + NY, NY) * 2 + c}

    def at_x(xx):
        return {"seq": lax.rem(xx + NX, NX) * NZ + z}

    def at_z(zz):
        return {"seq": x * NZ + lax.rem(zz + NZ, NZ)}

    partner = {"group": y * 2 + 1 - c}
    y_peer = (at_y(y + 1), at_y(y - 1))
    x_peer = (at_x(x + 1), at_x(x - 1))
    z_peer = (at_z(z + 1), at_z(z - 1))

    def remote(src, dst, send, recv, device):
        return pltpu.make_async_remote_copy(src, dst, send, recv, device_id=device, device_id_type=pl.DeviceIdType.MESH)

    def local_kv(h):
        return pltpu.make_async_copy(
            cache_ref.at[:, :, :, pl.ds(h * HEAD, HEAD)], kvs[h].at[:, :, x], lk.at[h]
        )

    has_queries = (y == 4) | (y == 5)
    my_rows = pl.ds(pl.multiple_of(z * ROWS, ROWS), ROWS)
    own_win = pltpu.make_async_copy(inw_ref, win.at[g], lw.at[0])
    own_part = pltpu.make_async_copy(inw_ref.at[my_rows, :], win.at[g, my_rows, :], lw.at[0])

    def own_weights(act):
        @pl.when(has_queries)
        def _():
            act(own_part)

        @pl.when(jnp.logical_not(has_queries))
        def _():
            act(own_win)

    own_wout = pltpu.make_async_copy(outw_ref, wout.at[g], lw.at[1])
    own_rows_in = pltpu.make_async_copy(cand_hbm, cand_ref, lw.at[2])
    local_kv(0).start()
    own_weights(lambda copy: copy.start())
    own_rows_in.start()
    for h in range(1, HEADS):
        local_kv(h).start()
    own_wout.start()

    barrier = pltpu.get_barrier_semaphore()
    for peer in (partner,) + x_peer + tuple(at_y(y + k) for k in range(1, NY)) + tuple(at_z(z + k) for k in range(1, NZ)):
        pl.semaphore_signal(barrier, inc=1, device_id=peer, device_id_type=pl.DeviceIdType.MESH)

    local_kv(0).wait()
    pl.semaphore_wait(barrier, 3 + NY - 1 + NZ - 1)

    def x_first(h, way):
        ref = kvs[h].at[:, :, x]
        return remote(ref, ref, xs.at[h, way], xr.at[h, way], x_peer[way])

    def x_second(h, way):
        block = lax.rem(x + (NX - 1 if way == 0 else 1), NX)
        ref = kvs[h].at[way, :, block]
        return remote(ref, ref, xs.at[h, 2 + way], xr.at[h, 2 + way], x_peer[way])

    def x_part(way, second):
        index = 1 - way if second else way
        ref = kvs[HEADS - 1].at[index, :, x]
        return remote(ref, ref, xs.at[HEADS - 1, way + 4 * second], xr.at[HEADS - 1, way + 4 * second], x_peer[way])

    def x_part_arrival(way, second):
        index = 1 - way if second else way
        block = lax.rem(x + (NX - 1 if way == 0 else 1), NX)
        ref = kvs[HEADS - 1].at[index, :, block]
        remote(ref, ref, xs.at[HEADS - 1, way + 4 * second], xr.at[HEADS - 1, way + 4 * second], x_peer[way]).wait_recv()

    def x_handle(h):
        for way in range(2):
            if h == HEADS - 1:
                x_part_arrival(way, 0)
            else:
                block = lax.rem(x + (NX - 1 if way == 0 else 1), NX)
                ref = kvs[h].at[:, :, block]
                remote(ref, ref, xs.at[h, way], xr.at[h, way], x_peer[way]).wait_recv()
            x_second(h, way).start()
        for way in range(2):
            if h + WINDOW < HEADS - 1:
                x_first(h + WINDOW, way).start()
            if h in (HEADS - 3, HEADS - 2):
                x_part(way, h - (HEADS - 3)).start()

    def x_complete(h):
        block = lax.rem(x + 2, NX)
        for way in range(2):
            if h == HEADS - 1:
                x_part_arrival(way, 1)
            ref = kvs[h].at[way, :, block]
            remote(ref, ref, xs.at[h, 2 + way], xr.at[h, 2 + way], x_peer[way]).wait_recv()

    def z_copy(hop, part, way):
        block = lax.rem(z + (NZ - hop if way == 0 else hop), NZ)
        start = pl.multiple_of(block * ROWS + part * (ROWS // 2), ROWS // 2)
        ref = nbuf.at[pl.ds(start, ROWS // 2), :]
        return remote(ref, ref, zs.at[min(hop, 3), part, way], zr.at[min(hop, 3), part, way], z_peer[way])

    def z_arrival(hop, part, way):
        block = lax.rem(z + (NZ - hop if way == 0 else hop), NZ)
        start = pl.multiple_of(block * ROWS + part * (ROWS // 2), ROWS // 2)
        ref = nbuf.at[pl.ds(start, ROWS // 2), :]
        return remote(ref, ref, zs.at[hop - 1, part, way], zr.at[hop - 1, part, way], z_peer[way])

    def z_sends(hop, part, way):
        return hop < 3 or (hop == 3 and part == way)

    def z_handle(hop, part):
        for way in range(2):
            if hop < 4 or part == way:
                z_arrival(hop, part, way).wait_recv()
            if z_sends(hop, part, way):
                z_copy(hop, part, way).start()

    def w_ref(b, piece, core):
        return win.at[2 * b + core, pl.ds(piece * PIECE, PIECE), :]

    def y_block(way, hop):
        return lax.rem(y + NY - hop if way == 0 else y + hop, NY)

    def y_sends(way, hop, piece):
        return hop < 3 or (hop == 3 and piece == way)

    def y_copy(way, hop, piece):
        ref = w_ref(y_block(way, hop), piece, c)
        return remote(ref, ref, ys.at[way, hop, piece], yr.at[way, hop, piece], y_peer[way])

    def y_cross(b, piece):
        ref = w_ref(b, piece, c)
        return remote(ref, ref, ycs.at[b, piece], ycr.at[b, piece], partner)

    def y_cross_arrival(b):
        for piece in range(PIECES):
            ref = w_ref(b, piece, 1 - c)
            remote(ref, ref, ycs.at[b, piece], ycr.at[b, piece], partner).wait_recv()

    def y_guard(way, hop):
        b = y_block(way, hop)
        return (b != 4) & (b != 5)

    def y_slot(hop, piece):
        for way in range(2):
            if hop > 0 and not y_sends(way, hop - 1, piece):
                continue

            @pl.when(y_guard(way, hop))
            def _():
                b = y_block(way, hop)
                if hop > 0:
                    ref = w_ref(b, piece, c)
                    remote(ref, ref, ys.at[way, hop - 1, piece], yr.at[way, hop - 1, piece], y_peer[way]).wait_recv()
                if y_sends(way, hop, piece):
                    y_copy(way, hop, piece).start()
                if hop > 0 or way == 0:
                    y_cross(b, piece).start()

    def q_part(b, way, hop):
        block = lax.rem(z + NZ - hop if way == 0 else z + hop, NZ)
        if hop < 3:
            return win.at[2 * b + c, pl.ds(pl.multiple_of(block * ROWS, ROWS), ROWS), :]
        start = pl.multiple_of(block * ROWS + way * (ROWS // 2), ROWS // 2)
        return win.at[2 * b + c, pl.ds(start, ROWS // 2), :]

    def q_far(b, k):
        ref = win.at[2 * b + c, my_rows, :]
        return remote(ref, ref, qs.at[b - 4, k], qr.at[b - 4], at_y(y + k))

    def q_share():
        for b in (4, 5):
            @pl.when(y == b)
            def _():
                for k in (4, 3, 5, 2, 6, 1, 7):
                    q_far(b, k).start()

    def q_copy(b, hop, way):
        ref = q_part(b, way, hop)
        return remote(ref, ref, qzs.at[b - 4, hop, way], qzr.at[b - 4, hop, way], z_peer[way])

    def q_slot(b, hop):
        if hop == 0:
            @pl.when(y != b)
            def _():
                q_far(b, 1).wait_recv()

        for way in range(2):
            if hop > 0:
                block = lax.rem(z + NZ - hop if way == 0 else z + hop, NZ)
                if hop < 4:
                    ref = win.at[2 * b + c, pl.ds(pl.multiple_of(block * ROWS, ROWS), ROWS), :]
                else:
                    start = pl.multiple_of(block * ROWS + way * (ROWS // 2), ROWS // 2)
                    ref = win.at[2 * b + c, pl.ds(start, ROWS // 2), :]
                remote(ref, ref, qzs.at[b - 4, hop - 1, way], qzr.at[b - 4, hop - 1, way], z_peer[way]).wait_recv()
            if hop < 4:
                q_copy(b, hop, way).start()
        if hop == 4:
            q_cross(b).start()

    def q_cross(b):
        ref = win.at[2 * b + c]
        return remote(ref, ref, qcs.at[b - 4], qcr.at[b - 4], partner)

    def q_cross_arrival(b):
        ref = win.at[2 * b + 1 - c]
        remote(ref, ref, qcs.at[b - 4], qcr.at[b - 4], partner).wait_recv()

    def o_copy(way, hop):
        ref = wout.at[2 * y_block(way, hop) + c]
        return remote(ref, ref, os.at[way, hop], orv.at[way, hop], y_peer[way])

    def o_cross(b):
        ref = wout.at[2 * b + c]
        return remote(ref, ref, ocs.at[b], ocr.at[b], partner)

    def o_slot(hop):
        for way in range(2):
            if hop == 4 and way == 1:
                continue
            b = y_block(way, hop)
            if hop > 0:
                ref = wout.at[2 * b + c]
                remote(ref, ref, os.at[way, hop - 1], orv.at[way, hop - 1], y_peer[way]).wait_recv()
            if hop < 3 or (hop == 3 and way == 0):
                o_copy(way, hop).start()
            if hop > 0 or way == 0:
                o_cross(b).start()

    def queries(block):
        @pl.loop(0, NZ // 2)
        def _(i):
            rows = pl.ds(pl.multiple_of(i * 2 * ROWS, 2 * ROWS), 2 * ROWS)
            value = jnp.dot(nbuf[rows, :], win[2 * 4 + block], preferred_element_type=jnp.float32)
            qbuf[rows, block * BLOCK : (block + 1) * BLOCK] = silu(value).astype(jnp.bfloat16)

    column = lax.broadcasted_iota(jnp.int32, (1, NX * SLOTS), 1)
    slot = (column // SLOTS * NZ + z) * SLOTS + column % SLOTS

    def send_partial(h, dest):
        return remote(snd.at[h, dest], rcv.at[h - RING, z], ss.at[h - RING, dest], rs.at[h - RING, z], at_z(dest))

    def attend(h):
        kv = kvs[h]

        def block(i):
            step = (i + 1) // 2
            dest = lax.rem(z + 4 + NZ + (1 - 2 * (i % 2)) * step, NZ)
            request = owner_ref[0, x * NZ + dest]
            length = len_ref[request]
            query = qbuf[pl.ds(pl.multiple_of(dest * ROWS, ROWS), ROWS), h * HEAD : (h + 1) * HEAD]
            keys = kv[0, request].reshape(NX * SLOTS, HEAD)
            values = kv[1, request].reshape(NX * SLOTS, HEAD)
            scores = lax.dot_general(
                query, keys, (((1,), (1,)), ((), ())), preferred_element_type=jnp.float32
            )
            weights = jnp.where(slot < length, silu(scores * factor), 0.0).astype(jnp.bfloat16)
            return dest, jnp.dot(weights, values, preferred_element_type=jnp.float32).astype(jnp.bfloat16)

        @pl.loop(0, NZ // UNROLL)
        def _(j):
            done = [block(j * UNROLL + k) for k in range(UNROLL)]
            for dest, part in done:
                snd[h, dest] = part
            if h >= RING:
                for k, (dest, _) in enumerate(done):
                    if k < UNROLL - 1:
                        send_partial(h, dest).start()
                    else:
                        @pl.when(j < NZ // UNROLL - 1)
                        def _():
                            send_partial(h, dest).start()

        if h < RING:
            ring_step(h, 1)
            pending[h] = 2

    def collect(h):
        total = acc[:, h * HEAD : (h + 1) * HEAD] + snd[h, z].astype(jnp.float32)
        for k in range(1, NZ):
            src = lax.rem(z + k, NZ)
            block = rcv.at[h - RING, src]
            remote(block, block, ss.at[h - RING, src], rs.at[h - RING, src], at_z(src)).wait_recv()
            total = total + rcv[h - RING, src].astype(jnp.float32)
        acc[:, h * HEAD : (h + 1) * HEAD] = total

    pending = {}

    def ring_rows(way, hop):
        return slice(0, ROWS) if hop > 1 else slice(0, ROWS // 2) if way == 0 else slice(ROWS // 2, ROWS)

    def ring_copy(h, hop, way):
        dest = lax.rem(z + 5 - hop if way == 0 else z + NZ - 5 + hop, NZ)
        rows = ring_rows(way, hop)
        return dest, remote(
            snd.at[h, dest, rows], rsb.at[way, h, hop - 1, rows], rss.at[way, h, hop - 1], rsr.at[way, h, hop - 1], z_peer[way]
        )

    def ring_take(h, hop, way):
        rows = ring_rows(way, hop)
        ref = rsb.at[way, h, hop - 1, rows]
        remote(ref, ref, rss.at[way, h, hop - 1], rsr.at[way, h, hop - 1], z_peer[way]).wait_recv()
        return rsb[way, h, hop - 1, rows].astype(jnp.float32)

    def ring_step(h, hop):
        for way in range(2):
            dest, copy = ring_copy(h, hop, way)
            if hop > 1:
                rows = ring_rows(way, hop - 1)
                total = snd[h, dest, rows].astype(jnp.float32) + ring_take(h, hop - 1, way)
                snd[h, dest, rows] = total.astype(jnp.bfloat16)
            copy.start()

    def tick():
        for h in sorted(pending):
            hop = pending[h]
            if hop <= 4:
                ring_step(h, hop)
                pending[h] = hop + 1
            else:
                columns = slice(h * HEAD, (h + 1) * HEAD)
                acc[:, columns] += snd[h, z].astype(jnp.float32) + ring_take(h, 4, 0) + ring_take(h, 4, 1)
                del pending[h]

    def own_rows():
        rows = pl.ds(pl.multiple_of(z * ROWS, ROWS), ROWS)
        mine = nbuf[rows, :]

        def project(block):
            value = jnp.dot(mine, win[block], preferred_element_type=jnp.float32)
            return silu(value).astype(jnp.bfloat16)

        for j in range(4):
            columns = slice(j * BLOCK, (j + 1) * BLOCK)
            ubuf[:, columns] = project(j)
            own_v = project(4 + j).astype(jnp.float32)
            own_k = project(12 + j).astype(jnp.float32)
            product = qbuf[rows, columns].astype(jnp.float32) * own_k
            for t in range(BLOCK // HEAD):
                part = slice(t * HEAD, (t + 1) * HEAD)
                score = jnp.sum(product[:, part], axis=-1, keepdims=True) * factor
                acc[:, j * BLOCK + t * HEAD : j * BLOCK + (t + 1) * HEAD] += silu(score) * own_v[:, part]

    own_weights(lambda copy: copy.wait())
    q_share()
    for way in range(2):
        x_first(0, way).start()
    own_wout.wait()
    y_slot(0, 0)
    o_slot(0)
    own_rows_in.wait()
    nbuf[my_rows, :] = layer_norm(cand_ref[...].astype(jnp.float32), ing_ref[...]).astype(jnp.bfloat16)
    for part in range(2):
        for way in range(2):
            z_copy(0, part, way).start()
    local_kv(1).wait()
    for way in range(2):
        x_first(1, way).start()
    acc[...] = jnp.zeros_like(acc)
    for h in range(2, HEADS):
        local_kv(h).wait()
    for way in range(2):
        x_first(2, way).start()
    y_slot(0, 1)
    z_handle(1, 0)
    z_handle(1, 1)
    q_slot(4, 0)
    x_handle(0)
    z_handle(2, 0)
    z_handle(2, 1)
    y_slot(1, 0)
    q_slot(4, 1)
    q_slot(4, 2)
    y_slot(1, 1)
    x_handle(1)
    z_handle(3, 0)
    z_handle(3, 1)
    q_slot(4, 3)
    q_slot(5, 0)
    z_handle(4, 0)
    z_handle(4, 1)
    q_slot(4, 4)
    q_slot(5, 1)
    y_slot(2, 0)
    x_handle(2)
    q_slot(5, 2)
    q_cross_arrival(4)
    queries(0)
    x_complete(0)
    attend(0)
    q_slot(5, 3)
    y_slot(2, 1)
    queries(1)
    x_complete(1)
    tick()
    attend(1)
    q_slot(5, 4)
    x_handle(3)
    y_slot(3, 0)
    x_complete(2)
    tick()
    attend(2)
    o_slot(1)
    q_cross_arrival(5)
    queries(2)
    queries(3)
    y_slot(3, 1)
    x_handle(4)
    x_complete(3)
    tick()
    attend(3)
    o_slot(2)
    y_slot(4, 0)
    y_slot(4, 1)
    x_handle(5)
    x_complete(4)
    tick()
    attend(4)
    o_slot(3)
    for b in range(NY):
        if b not in (4, 5):
            y_cross_arrival(b)
    own_rows()
    o_slot(4)
    x_handle(6)
    x_complete(5)
    tick()
    attend(5)
    x_handle(7)
    for h in range(RING, 5):
        collect(h)
    for b in range(NY):
        remote(wout.at[2 * b + 1 - c], wout.at[2 * b + 1 - c], ocs.at[b], ocr.at[b], partner).wait_recv()
    x_complete(6)
    attend(6)
    tick()
    collect(5)
    x_complete(7)
    attend(7)
    while pending:
        tick()
    collect(6)
    collect(7)
    gated = (layer_norm(acc[...], outg_ref[...]) * ubuf[...].astype(jnp.float32)).astype(jnp.bfloat16)
    result = jnp.dot(gated, wout[...].reshape(D, D), preferred_element_type=jnp.float32)
    out_ref[...] = (cand_ref[...].astype(jnp.float32) + result).astype(jnp.bfloat16)

    for h in range(HEADS):
        for way in range(2):
            x_second(h, way).wait_send()
            if h < HEADS - 1:
                x_first(h, way).wait_send()
            else:
                x_part(way, 0).wait_send()
                x_part(way, 1).wait_send()
    for hop in range(4):
        for part in range(2):
            for way in range(2):
                if z_sends(hop, part, way):
                    z_copy(hop, part, way).wait_send()
    for way in range(2):
        for hop in range(4):
            @pl.when(y_guard(way, hop))
            def _():
                for piece in range(PIECES):
                    if y_sends(way, hop, piece):
                        y_copy(way, hop, piece).wait_send()

            if hop < 3 or way == 0:
                o_copy(way, hop).wait_send()
            for b in (4, 5):
                q_copy(b, hop, way).wait_send()
    for b in range(NY):
        o_cross(b).wait_send()
        if b in (4, 5):
            q_cross(b).wait_send()

            @pl.when(y == b)
            def _():
                for k in range(1, NY):
                    q_far(b, k).wait_send()
        else:
            for piece in range(PIECES):
                y_cross(b, piece).wait_send()
    for h in range(RING):
        for hop in range(1, 5):
            for way in range(2):
                ring_copy(h, hop, way)[1].wait_send()

    for h in range(RING, HEADS):
        @pl.loop(1, NZ)
        def _(k):
            send_partial(h, lax.rem(z + k, NZ)).wait_send()


def local(cand_x, in_weight, out_weight, in_gain, out_gain, cache_kv, hist_len, owner):
    bf16, dma = jnp.bfloat16, pltpu.SemaphoreType.DMA
    vmem, anywhere = pl.BlockSpec(memory_space=pltpu.VMEM), pl.BlockSpec(memory_space=pl.ANY)
    smem = pl.BlockSpec(memory_space=pltpu.SMEM)
    return pl.pallas_call(
        kernel,
        out_shape=jax.ShapeDtypeStruct((ROWS, D), bf16),
        in_specs=[anywhere, anywhere, anywhere, vmem, vmem, anywhere, smem, smem],
        out_specs=vmem,
        scratch_shapes=[pltpu.VMEM((2, REQ, NX, SLOTS, HEAD), bf16) for _ in range(HEADS)]
        + [
            pltpu.VMEM((ROWS, D), bf16),
            pltpu.VMEM((2 * NY, D, BLOCK), bf16),
            pltpu.VMEM((2 * NY, D // (2 * NY), D), bf16),
            pltpu.VMEM((NZ * ROWS, D), bf16),
            pltpu.VMEM((NZ * ROWS, D), bf16),
            pltpu.VMEM((ROWS, D), bf16),
            pltpu.VMEM((HEADS, NZ, ROWS, HEAD), bf16),
            pltpu.VMEM((max(HEADS - RING, 1), NZ, ROWS, HEAD), bf16),
            pltpu.VMEM((ROWS, D), jnp.float32),
            pltpu.VMEM((2, max(RING, 1), 4, ROWS, HEAD), bf16),
            dma((HEADS,)), dma((3,)),
            dma((HEADS, 6)), dma((HEADS, 6)),
            dma((4, 2, 2)), dma((4, 2, 2)),
            dma((2, 4, PIECES)), dma((2, 4, PIECES)), dma((NY, PIECES)), dma((NY, PIECES)),
            dma((2, NY)), dma((2,)), dma((2, 4, 2)), dma((2, 4, 2)), dma((2,)), dma((2,)),
            dma((2, 4)), dma((2, 4)), dma((NY,)), dma((NY,)),
            dma((max(HEADS - RING, 1), NZ)), dma((max(HEADS - RING, 1), NZ)),
            dma((2, max(RING, 1), 4)), dma((2, max(RING, 1), 4)),
        ],
        compiler_params=pltpu.CompilerParams(
            collective_id=0, has_side_effects=True, vmem_limit_bytes=56 * 1024 * 1024
        ),
        cost_estimate=pl.CostEstimate(flops=5_000_000_000, bytes_accessed=4_000_000, transcendentals=4_000_000),
    )(cand_x, in_weight, out_weight, in_gain[None, :], out_gain[None, :], cache_kv, hist_len, owner)


def solution(mesh):
    placed = (
        P(("group", "seq"), None),
        P(None, "group"),
        P("group", None),
        P(),
        P(),
        P(None, "group", "seq", None),
        P("group"),
        P("group", None),
    )
    return jax.shard_map(
        local, mesh=mesh, in_specs=placed, out_specs=P(("group", "seq"), None), check_vma=False
    )
```

```python
import math

import jax
import jax.numpy as jnp
from jax import lax
from jax.experimental import pallas as pl
from jax.experimental.pallas import tpu as pltpu
from jax.sharding import PartitionSpec as P

HEADS = 8
HEAD = 128
NY, NX, NZ = 8, 4, 8
PIECES = 2
ROWS = 128
D = 1024
BLOCK = 256
SLOTS = 64
REQ = 8
PIECE = D // PIECES
WINDOW = 3
UNROLL = 2
RING = 2


def silu(v):
    half = 0.5 * v
    return half + half * jnp.tanh(half)


def layer_norm(values_in, gain):
    centre = jnp.mean(values_in, axis=-1, keepdims=True)
    centred = values_in - centre
    spread = jnp.mean(centred * centred, axis=-1, keepdims=True)
    return centred * lax.rsqrt(spread + 1e-05) * gain


def kernel(cand_hbm, inw_ref, outw_ref, ing_ref, outg_ref, cache_ref, len_ref, owner_ref, out_ref, *scratch):
    kvs = scratch[:HEADS]
    (cand_ref, win, wout, nbuf, qbuf, ubuf, snd, rcv, acc,
     rsb,
     lk, lw, xs, xr, zs, zr, ys, yr, ycs, ycr, qs, qr, qzs, qzr, qcs, qcr, os, orv, ocs, ocr, ss, rs, rss, rsr) = scratch[HEADS:]
    g = lax.axis_index("group")
    s = lax.axis_index("seq")
    y, c = g // 2, g % 2
    x, z = s // NZ, s % NZ
    factor = 1.0 / math.sqrt(HEAD)

    def at_y(yy):
        return {"group": lax.rem(yy + NY, NY) * 2 + c}

    def at_x(xx):
        return {"seq": lax.rem(xx + NX, NX) * NZ + z}

    def at_z(zz):
        return {"seq": x * NZ + lax.rem(zz + NZ, NZ)}

    partner = {"group": y * 2 + 1 - c}
    y_peer = (at_y(y + 1), at_y(y - 1))
    x_peer = (at_x(x + 1), at_x(x - 1))
    z_peer = (at_z(z + 1), at_z(z - 1))

    def remote(src, dst, send, recv, device):
        return pltpu.make_async_remote_copy(src, dst, send, recv, device_id=device, device_id_type=pl.DeviceIdType.MESH)

    barrier = pltpu.get_barrier_semaphore()
    for peer in (partner,) + x_peer + y_peer + tuple(at_z(z + k) for k in range(1, NZ)):
        pl.semaphore_signal(barrier, inc=1, device_id=peer, device_id_type=pl.DeviceIdType.MESH)

    for b in (4, 5):
        @pl.when((y < b - 1) | (y > b + 1))
        def _():
            pl.semaphore_signal(barrier, inc=1, device_id=at_y(b), device_id_type=pl.DeviceIdType.MESH)

    def local_kv(h):
        return pltpu.make_async_copy(
            cache_ref.at[:, :, :, pl.ds(h * HEAD, HEAD)], kvs[h].at[:, :, x], lk.at[h]
        )

    has_queries = (y == 4) | (y == 5)
    my_rows = pl.ds(pl.multiple_of(z * ROWS, ROWS), ROWS)
    own_win = pltpu.make_async_copy(inw_ref, win.at[g], lw.at[0])
    own_part = pltpu.make_async_copy(inw_ref.at[my_rows, :], win.at[g, my_rows, :], lw.at[0])

    def own_weights(act):
        @pl.when(has_queries)
        def _():
            act(own_part)

        @pl.when(jnp.logical_not(has_queries))
        def _():
            act(own_win)

    own_wout = pltpu.make_async_copy(outw_ref, wout.at[g], lw.at[1])
    own_rows_in = pltpu.make_async_copy(cand_hbm, cand_ref, lw.at[2])
    local_kv(0).start()
    own_weights(lambda copy: copy.start())
    own_rows_in.start()
    for h in range(1, HEADS):
        local_kv(h).start()
    own_wout.start()

    local_kv(0).wait()
    pl.semaphore_wait(barrier, jnp.where((y == 4) | (y == 5), 3 + NY - 1 + NZ - 1, 5 + NZ - 1))

    def x_first(h, way):
        ref = kvs[h].at[:, :, x]
        return remote(ref, ref, xs.at[h, way], xr.at[h, way], x_peer[way])

    def x_second(h, way):
        block = lax.rem(x + (NX - 1 if way == 0 else 1), NX)
        ref = kvs[h].at[way, :, block]
        return remote(ref, ref, xs.at[h, 2 + way], xr.at[h, 2 + way], x_peer[way])

    def x_part(way, second):
        index = 1 - way if second else way
        ref = kvs[HEADS - 1].at[index, :, x]
        return remote(ref, ref, xs.at[HEADS - 1, way + 4 * second], xr.at[HEADS - 1, way + 4 * second], x_peer[way])

    def x_part_arrival(way, second):
        index = 1 - way if second else way
        block = lax.rem(x + (NX - 1 if way == 0 else 1), NX)
        ref = kvs[HEADS - 1].at[index, :, block]
        remote(ref, ref, xs.at[HEADS - 1, way + 4 * second], xr.at[HEADS - 1, way + 4 * second], x_peer[way]).wait_recv()

    def x_handle(h):
        for way in range(2):
            if h == HEADS - 1:
                x_part_arrival(way, 0)
            else:
                block = lax.rem(x + (NX - 1 if way == 0 else 1), NX)
                ref = kvs[h].at[:, :, block]
                remote(ref, ref, xs.at[h, way], xr.at[h, way], x_peer[way]).wait_recv()
            x_second(h, way).start()
        for way in range(2):
            if h + WINDOW < HEADS - 1:
                x_first(h + WINDOW, way).start()
            if h in (HEADS - 3, HEADS - 2):
                x_part(way, h - (HEADS - 3)).start()

    def x_complete(h):
        block = lax.rem(x + 2, NX)
        for way in range(2):
            if h == HEADS - 1:
                x_part_arrival(way, 1)
            ref = kvs[h].at[way, :, block]
            remote(ref, ref, xs.at[h, 2 + way], xr.at[h, 2 + way], x_peer[way]).wait_recv()

    def z_copy(hop, part, way):
        block = lax.rem(z + (NZ - hop if way == 0 else hop), NZ)
        start = pl.multiple_of(block * ROWS + part * (ROWS // 2), ROWS // 2)
        ref = nbuf.at[pl.ds(start, ROWS // 2), :]
        return remote(ref, ref, zs.at[min(hop, 3), part, way], zr.at[min(hop, 3), part, way], z_peer[way])

    def z_arrival(hop, part, way):
        block = lax.rem(z + (NZ - hop if way == 0 else hop), NZ)
        start = pl.multiple_of(block * ROWS + part * (ROWS // 2), ROWS // 2)
        ref = nbuf.at[pl.ds(start, ROWS // 2), :]
        return remote(ref, ref, zs.at[hop - 1, part, way], zr.at[hop - 1, part, way], z_peer[way])

    def z_sends(hop, part, way):
        return hop < 3 or (hop == 3 and part == way)

    def z_handle(hop, part):
        for way in range(2):
            if hop < 4 or part == way:
                z_arrival(hop, part, way).wait_recv()
            if z_sends(hop, part, way):
                z_copy(hop, part, way).start()

    def w_ref(b, piece, core):
        return win.at[2 * b + core, pl.ds(piece * PIECE, PIECE), :]

    def y_block(way, hop):
        return lax.rem(y + NY - hop if way == 0 else y + hop, NY)

    def y_sends(way, hop, piece):
        return hop < 3 or (hop == 3 and piece == way)

    def y_copy(way, hop, piece):
        ref = w_ref(y_block(way, hop), piece, c)
        return remote(ref, ref, ys.at[way, hop, piece], yr.at[way, hop, piece], y_peer[way])

    def y_cross(b, piece):
        ref = w_ref(b, piece, c)
        return remote(ref, ref, ycs.at[b, piece], ycr.at[b, piece], partner)

    def y_cross_arrival(b):
        for piece in range(PIECES):
            ref = w_ref(b, piece, 1 - c)
            remote(ref, ref, ycs.at[b, piece], ycr.at[b, piece], partner).wait_recv()

    def y_guard(way, hop):
        b = y_block(way, hop)
        return (b != 4) & (b != 5)

    def y_slot(hop, piece):
        for way in range(2):
            if hop > 0 and not y_sends(way, hop - 1, piece):
                continue

            @pl.when(y_guard(way, hop))
            def _():
                b = y_block(way, hop)
                if hop > 0:
                    ref = w_ref(b, piece, c)
                    remote(ref, ref, ys.at[way, hop - 1, piece], yr.at[way, hop - 1, piece], y_peer[way]).wait_recv()
                if y_sends(way, hop, piece):
                    y_copy(way, hop, piece).start()
                if hop > 0 or way == 0:
                    y_cross(b, piece).start()

    def q_part(b, way, hop):
        block = lax.rem(z + NZ - hop if way == 0 else z + hop, NZ)
        if hop < 3:
            return win.at[2 * b + c, pl.ds(pl.multiple_of(block * ROWS, ROWS), ROWS), :]
        start = pl.multiple_of(block * ROWS + way * (ROWS // 2), ROWS // 2)
        return win.at[2 * b + c, pl.ds(start, ROWS // 2), :]

    def q_far(b, k):
        ref = win.at[2 * b + c, my_rows, :]
        return remote(ref, ref, qs.at[b - 4, k], qr.at[b - 4], at_y(y + k))

    def q_share():
        for b in (4, 5):
            @pl.when(y == b)
            def _():
                for k in (4, 3, 5, 2, 6, 1, 7):
                    q_far(b, k).start()

    def q_copy(b, hop, way):
        ref = q_part(b, way, hop)
        return remote(ref, ref, qzs.at[b - 4, hop, way], qzr.at[b - 4, hop, way], z_peer[way])

    def q_slot(b, hop):
        if hop == 0:
            @pl.when(y != b)
            def _():
                q_far(b, 1).wait_recv()

        for way in range(2):
            if hop > 0:
                block = lax.rem(z + NZ - hop if way == 0 else z + hop, NZ)
                if hop < 4:
                    ref = win.at[2 * b + c, pl.ds(pl.multiple_of(block * ROWS, ROWS), ROWS), :]
                else:
                    start = pl.multiple_of(block * ROWS + way * (ROWS // 2), ROWS // 2)
                    ref = win.at[2 * b + c, pl.ds(start, ROWS // 2), :]
                remote(ref, ref, qzs.at[b - 4, hop - 1, way], qzr.at[b - 4, hop - 1, way], z_peer[way]).wait_recv()
            if hop < 4:
                q_copy(b, hop, way).start()
        if hop == 4:
            q_cross(b).start()

    def q_cross(b):
        ref = win.at[2 * b + c]
        return remote(ref, ref, qcs.at[b - 4], qcr.at[b - 4], partner)

    def q_cross_arrival(b):
        ref = win.at[2 * b + 1 - c]
        remote(ref, ref, qcs.at[b - 4], qcr.at[b - 4], partner).wait_recv()

    def o_copy(way, hop):
        ref = wout.at[2 * y_block(way, hop) + c]
        return remote(ref, ref, os.at[way, hop], orv.at[way, hop], y_peer[way])

    def o_cross(b):
        ref = wout.at[2 * b + c]
        return remote(ref, ref, ocs.at[b], ocr.at[b], partner)

    def o_slot(hop):
        for way in range(2):
            if hop == 4 and way == 1:
                continue
            b = y_block(way, hop)
            if hop > 0:
                ref = wout.at[2 * b + c]
                remote(ref, ref, os.at[way, hop - 1], orv.at[way, hop - 1], y_peer[way]).wait_recv()
            if hop < 3 or (hop == 3 and way == 0):
                o_copy(way, hop).start()
            if hop > 0 or way == 0:
                o_cross(b).start()

    def queries(block):
        @pl.loop(0, NZ // 2)
        def _(i):
            rows = pl.ds(pl.multiple_of(i * 2 * ROWS, 2 * ROWS), 2 * ROWS)
            value = jnp.dot(nbuf[rows, :], win[2 * 4 + block], preferred_element_type=jnp.float32)
            qbuf[rows, block * BLOCK : (block + 1) * BLOCK] = silu(value).astype(jnp.bfloat16)

    column = lax.broadcasted_iota(jnp.int32, (1, NX * SLOTS), 1)
    slot = (column // SLOTS * NZ + z) * SLOTS + column % SLOTS

    def send_partial(h, dest):
        return remote(snd.at[h, dest], rcv.at[h - RING, z], ss.at[h - RING, dest], rs.at[h - RING, z], at_z(dest))

    def attend(h):
        kv = kvs[h]

        def block(i):
            step = (i + 1) // 2
            dest = lax.rem(z + 4 + NZ + (1 - 2 * (i % 2)) * step, NZ)
            request = owner_ref[0, x * NZ + dest]
            length = len_ref[request]
            query = qbuf[pl.ds(pl.multiple_of(dest * ROWS, ROWS), ROWS), h * HEAD : (h + 1) * HEAD]
            keys = kv[0, request].reshape(NX * SLOTS, HEAD)
            values = kv[1, request].reshape(NX * SLOTS, HEAD)
            scores = lax.dot_general(
                query, keys, (((1,), (1,)), ((), ())), preferred_element_type=jnp.float32
            )
            weights = jnp.where(slot < length, silu(scores * factor), 0.0).astype(jnp.bfloat16)
            return dest, jnp.dot(weights, values, preferred_element_type=jnp.float32).astype(jnp.bfloat16)

        @pl.loop(0, NZ // UNROLL)
        def _(j):
            done = [block(j * UNROLL + k) for k in range(UNROLL)]
            for dest, part in done:
                snd[h, dest] = part
            if h >= RING:
                for k, (dest, _) in enumerate(done):
                    if k < UNROLL - 1:
                        send_partial(h, dest).start()
                    else:
                        @pl.when(j < NZ // UNROLL - 1)
                        def _():
                            send_partial(h, dest).start()

        if h < RING:
            ring_step(h, 1)
            pending[h] = 2

    def collect(h):
        total = acc[:, h * HEAD : (h + 1) * HEAD] + snd[h, z].astype(jnp.float32)
        for k in range(1, NZ):
            src = lax.rem(z + k, NZ)
            block = rcv.at[h - RING, src]
            remote(block, block, ss.at[h - RING, src], rs.at[h - RING, src], at_z(src)).wait_recv()
            total = total + rcv[h - RING, src].astype(jnp.float32)
        acc[:, h * HEAD : (h + 1) * HEAD] = total

    pending = {}

    def ring_rows(way, hop):
        return slice(0, ROWS) if hop > 1 else slice(0, ROWS // 2) if way == 0 else slice(ROWS // 2, ROWS)

    def ring_copy(h, hop, way):
        dest = lax.rem(z + 5 - hop if way == 0 else z + NZ - 5 + hop, NZ)
        rows = ring_rows(way, hop)
        return dest, remote(
            snd.at[h, dest, rows], rsb.at[way, h, hop - 1, rows], rss.at[way, h, hop - 1], rsr.at[way, h, hop - 1], z_peer[way]
        )

    def ring_take(h, hop, way):
        rows = ring_rows(way, hop)
        ref = rsb.at[way, h, hop - 1, rows]
        remote(ref, ref, rss.at[way, h, hop - 1], rsr.at[way, h, hop - 1], z_peer[way]).wait_recv()
        return rsb[way, h, hop - 1, rows].astype(jnp.float32)

    def ring_step(h, hop):
        for way in range(2):
            dest, copy = ring_copy(h, hop, way)
            if hop > 1:
                rows = ring_rows(way, hop - 1)
                total = snd[h, dest, rows].astype(jnp.float32) + ring_take(h, hop - 1, way)
                snd[h, dest, rows] = total.astype(jnp.bfloat16)
            copy.start()

    def tick():
        for h in sorted(pending):
            hop = pending[h]
            if hop <= 4:
                ring_step(h, hop)
                pending[h] = hop + 1
            else:
                columns = slice(h * HEAD, (h + 1) * HEAD)
                acc[:, columns] += snd[h, z].astype(jnp.float32) + ring_take(h, 4, 0) + ring_take(h, 4, 1)
                del pending[h]

    def own_rows():
        rows = pl.ds(pl.multiple_of(z * ROWS, ROWS), ROWS)
        mine = nbuf[rows, :]

        def project(block):
            value = jnp.dot(mine, win[block], preferred_element_type=jnp.float32)
            return silu(value).astype(jnp.bfloat16)

        for j in range(4):
            columns = slice(j * BLOCK, (j + 1) * BLOCK)
            ubuf[:, columns] = project(j)
            own_v = project(4 + j).astype(jnp.float32)
            own_k = project(12 + j).astype(jnp.float32)
            product = qbuf[rows, columns].astype(jnp.float32) * own_k
            for t in range(BLOCK // HEAD):
                part = slice(t * HEAD, (t + 1) * HEAD)
                score = jnp.sum(product[:, part], axis=-1, keepdims=True) * factor
                acc[:, j * BLOCK + t * HEAD : j * BLOCK + (t + 1) * HEAD] += silu(score) * own_v[:, part]

    own_weights(lambda copy: copy.wait())
    q_share()
    for way in range(2):
        x_first(0, way).start()
    own_wout.wait()
    y_slot(0, 0)
    o_slot(0)
    own_rows_in.wait()
    nbuf[my_rows, :] = layer_norm(cand_ref[...].astype(jnp.float32), ing_ref[...]).astype(jnp.bfloat16)
    for part in range(2):
        for way in range(2):
            z_copy(0, part, way).start()
    local_kv(1).wait()
    for way in range(2):
        x_first(1, way).start()
    acc[...] = jnp.zeros_like(acc)
    for h in range(2, HEADS):
        local_kv(h).wait()
    for way in range(2):
        x_first(2, way).start()
    y_slot(0, 1)
    z_handle(1, 0)
    z_handle(1, 1)
    q_slot(4, 0)
    x_handle(0)
    z_handle(2, 0)
    z_handle(2, 1)
    y_slot(1, 0)
    q_slot(4, 1)
    q_slot(4, 2)
    y_slot(1, 1)
    x_handle(1)
    z_handle(3, 0)
    z_handle(3, 1)
    q_slot(4, 3)
    q_slot(5, 0)
    z_handle(4, 0)
    z_handle(4, 1)
    q_slot(4, 4)
    q_slot(5, 1)
    y_slot(2, 0)
    x_handle(2)
    q_slot(5, 2)
    q_cross_arrival(4)
    queries(0)
    x_complete(0)
    attend(0)
    q_slot(5, 3)
    y_slot(2, 1)
    queries(1)
    x_complete(1)
    tick()
    attend(1)
    q_slot(5, 4)
    x_handle(3)
    y_slot(3, 0)
    x_complete(2)
    tick()
    attend(2)
    o_slot(1)
    q_cross_arrival(5)
    queries(2)
    queries(3)
    y_slot(3, 1)
    x_handle(4)
    x_complete(3)
    tick()
    attend(3)
    o_slot(2)
    y_slot(4, 0)
    y_slot(4, 1)
    x_handle(5)
    x_complete(4)
    tick()
    attend(4)
    o_slot(3)
    for b in range(NY):
        if b not in (4, 5):
            y_cross_arrival(b)
    own_rows()
    o_slot(4)
    x_handle(6)
    x_complete(5)
    tick()
    attend(5)
    x_handle(7)
    for h in range(RING, 5):
        collect(h)
    for b in range(NY):
        remote(wout.at[2 * b + 1 - c], wout.at[2 * b + 1 - c], ocs.at[b], ocr.at[b], partner).wait_recv()
    x_complete(6)
    attend(6)
    tick()
    collect(5)
    x_complete(7)
    attend(7)
    while pending:
        tick()
    collect(6)
    collect(7)
    gated = (layer_norm(acc[...], outg_ref[...]) * ubuf[...].astype(jnp.float32)).astype(jnp.bfloat16)
    result = jnp.dot(gated, wout[...].reshape(D, D), preferred_element_type=jnp.float32)
    out_ref[...] = (cand_ref[...].astype(jnp.float32) + result).astype(jnp.bfloat16)

    for h in range(HEADS):
        for way in range(2):
            x_second(h, way).wait_send()
            if h < HEADS - 1:
                x_first(h, way).wait_send()
            else:
                x_part(way, 0).wait_send()
                x_part(way, 1).wait_send()
    for hop in range(4):
        for part in range(2):
            for way in range(2):
                if z_sends(hop, part, way):
                    z_copy(hop, part, way).wait_send()
    for way in range(2):
        for hop in range(4):
            @pl.when(y_guard(way, hop))
            def _():
                for piece in range(PIECES):
                    if y_sends(way, hop, piece):
                        y_copy(way, hop, piece).wait_send()

            if hop < 3 or way == 0:
                o_copy(way, hop).wait_send()
            for b in (4, 5):
                q_copy(b, hop, way).wait_send()
    for b in range(NY):
        o_cross(b).wait_send()
        if b in (4, 5):
            q_cross(b).wait_send()

            @pl.when(y == b)
            def _():
                for k in range(1, NY):
                    q_far(b, k).wait_send()
        else:
            for piece in range(PIECES):
                y_cross(b, piece).wait_send()
    for h in range(RING):
        for hop in range(1, 5):
            for way in range(2):
                ring_copy(h, hop, way)[1].wait_send()

    for h in range(RING, HEADS):
        @pl.loop(1, NZ)
        def _(k):
            send_partial(h, lax.rem(z + k, NZ)).wait_send()


def local(cand_x, in_weight, out_weight, in_gain, out_gain, cache_kv, hist_len, owner):
    bf16, dma = jnp.bfloat16, pltpu.SemaphoreType.DMA
    vmem, anywhere = pl.BlockSpec(memory_space=pltpu.VMEM), pl.BlockSpec(memory_space=pl.ANY)
    smem = pl.BlockSpec(memory_space=pltpu.SMEM)
    return pl.pallas_call(
        kernel,
        out_shape=jax.ShapeDtypeStruct((ROWS, D), bf16),
        in_specs=[anywhere, anywhere, anywhere, vmem, vmem, anywhere, smem, smem],
        out_specs=vmem,
        scratch_shapes=[pltpu.VMEM((2, REQ, NX, SLOTS, HEAD), bf16) for _ in range(HEADS)]
        + [
            pltpu.VMEM((ROWS, D), bf16),
            pltpu.VMEM((2 * NY, D, BLOCK), bf16),
            pltpu.VMEM((2 * NY, D // (2 * NY), D), bf16),
            pltpu.VMEM((NZ * ROWS, D), bf16),
            pltpu.VMEM((NZ * ROWS, D), bf16),
            pltpu.VMEM((ROWS, D), bf16),
            pltpu.VMEM((HEADS, NZ, ROWS, HEAD), bf16),
            pltpu.VMEM((max(HEADS - RING, 1), NZ, ROWS, HEAD), bf16),
            pltpu.VMEM((ROWS, D), jnp.float32),
            pltpu.VMEM((2, max(RING, 1), 4, ROWS, HEAD), bf16),
            dma((HEADS,)), dma((3,)),
            dma((HEADS, 6)), dma((HEADS, 6)),
            dma((4, 2, 2)), dma((4, 2, 2)),
            dma((2, 4, PIECES)), dma((2, 4, PIECES)), dma((NY, PIECES)), dma((NY, PIECES)),
            dma((2, NY)), dma((2,)), dma((2, 4, 2)), dma((2, 4, 2)), dma((2,)), dma((2,)),
            dma((2, 4)), dma((2, 4)), dma((NY,)), dma((NY,)),
            dma((max(HEADS - RING, 1), NZ)), dma((max(HEADS - RING, 1), NZ)),
            dma((2, max(RING, 1), 4)), dma((2, max(RING, 1), 4)),
        ],
        compiler_params=pltpu.CompilerParams(
            collective_id=0, has_side_effects=True, vmem_limit_bytes=56 * 1024 * 1024
        ),
        cost_estimate=pl.CostEstimate(flops=5_000_000_000, bytes_accessed=4_000_000, transcendentals=4_000_000),
    )(cand_x, in_weight, out_weight, in_gain[None, :], out_gain[None, :], cache_kv, hist_len, owner)


def solution(mesh):
    placed = (
        P(("group", "seq"), None),
        P(None, "group"),
        P("group", None),
        P(),
        P(),
        P(None, "group", "seq", None),
        P("group"),
        P("group", None),
    )
    return jax.shard_map(
        local, mesh=mesh, in_specs=placed, out_specs=P(("group", "seq"), None), check_vma=False
    )
```
